512 devices in a mesh: grp: 16 (over x, y), batch: 8 (over z_lo), tp: 4 (over z_hi, core).
Axes of the slice: x: 4, y: 4, z: 16 (z_hi: 2, z_lo: 8; z = z_hi * 8 + z_lo), core: 2. Of those that a mesh axis runs over, the one named last changes fastest.
Arguments:
- prefix_q: bfloat16 [8192, 8192], P(('batch', 'grp'), 'tp'), parts along dimension 0, may hold values from -6 to 6
- prefix_k: bfloat16 [8192, 1024], P(('batch', 'grp'), 'tp'), parts along dimension 0, may hold values from -6 to 6
- prefix_v: bfloat16 [8192, 1024], P(('batch', 'grp'), 'tp'), parts along dimension 0, may hold values from -6 to 6
- resp_q: bfloat16 [128, 128, 8192], P(('batch', 'grp'), None, 'tp'), parts along dimension 0, may hold values from -6 to 6
- resp_k: bfloat16 [128, 128, 1024], P(('batch', 'grp'), None, 'tp'), parts along dimension 0, may hold values from -6 to 6
- resp_v: bfloat16 [128, 128, 1024], P(('batch', 'grp'), None, 'tp'), parts along dimension 0, may hold values from -6 to 6
- lengths: int32 [128], P(('batch', 'grp')), parts along dimension 0, may hold values from 64 to 128, as said below
- d_prefix_out: bfloat16 [8192, 8192], P(('batch', 'grp'), 'tp'), parts along dimension 0, may hold values from -6 to 6
- d_resp_out: bfloat16 [128, 128, 8192], P(('batch', 'grp'), None, 'tp'), parts along dimension 0, may hold values from -6 to 6
Outputs:
- grad_prefix_q: bfloat16 [8192, 8192], P(('batch', 'grp'), 'tp'), parts along dimension 0
- grad_prefix_k: bfloat16 [8192, 1024], P(('batch', 'grp'), 'tp'), parts along dimension 0
- grad_prefix_v: bfloat16 [8192, 1024], P(('batch', 'grp'), 'tp'), parts along dimension 0
- grad_resp_q: bfloat16 [128, 128, 8192], P(('batch', 'grp'), None, 'tp'), parts along dimension 0
- grad_resp_k: bfloat16 [128, 128, 1024], P(('batch', 'grp'), None, 'tp'), parts along dimension 0
- grad_resp_v: bfloat16 [128, 128, 1024], P(('batch', 'grp'), None, 'tp'), parts along dimension 0
The draws below stay inside these ranges and needn't reach their ends.
There are 8 independent parts, one for each index of `batch`. The reference program is written for one: setup_inputs(seed, part) draws one part's arguments, and reference() takes and returns one part's arrays. A program takes and returns all parts, laid end to end along the dimension named above; each array names one. Nothing has to cross between parts.
Inputs may be any that keep to these rules, and one draw needn't show every extreme that they name: `lengths`: each response's length; some response has exactly 128 tokens in every draw.
All inputs are finite; a program needn't handle non-finite values.
Results may differ from the reference program's by a relative error of at most 0.019.
Values may be sent and summed in bfloat16 or wider, within the bound.
No kernel may reach another device: no remote copies, remote signals or barrier semaphores. Data moves between devices by JAX's collectives and lax.ppermute only.
A program may use at most 64 MiB of HBM per device.

```python
import math
import jax
import jax.numpy as jnp
from jax import lax

HQ = 64
KVH = 8
HD = 128
R_MAX = 128
PREFIX = 1024
N_GRP = 16


def draw_prefix_k(key, part):
    key = jax.random.fold_in(key, 21)
    shape = (PREFIX, KVH * HD)
    field = jnp.clip(jax.random.normal(key, shape, jnp.float32), -5.0, 5.0)
    return field.astype(jnp.bfloat16)


def draw_prefix_q(key, part):
    key = jax.random.fold_in(key, 22)
    shape = (PREFIX, HQ * HD)
    field = jnp.clip(jax.random.normal(key, shape, jnp.float32), -5.0, 5.0)
    return field.astype(jnp.bfloat16)


def draw_resp_q(key, part):
    key = jax.random.fold_in(key, 23)
    shape = (N_GRP, R_MAX, HQ * HD)
    field = jnp.clip(jax.random.normal(key, shape, jnp.float32), -5.0, 5.0)
    return field.astype(jnp.bfloat16)


def draw_lengths(key, part):
    key = jax.random.fold_in(key, 24)
    first_key, second_key = jax.random.split(key)
    base_lengths = jax.random.randint(first_key, (N_GRP,), R_MAX // 2, R_MAX + 1)
    longest = jax.random.randint(second_key, (), 0, N_GRP)
    return jnp.where(jnp.arange(N_GRP) == longest, R_MAX, base_lengths).astype(jnp.int32)


def shard_levels(stream_key, extent, cuts, smallest, largest):
    level = 1.0
    for axis_at, shards_of in cuts:
        draws = jax.random.uniform(jax.random.fold_in(jax.random.fold_in(stream_key, 6), axis_at), (shards_of,), jnp.float32, smallest / len(cuts), largest / len(cuts))
        level = level * jnp.repeat(jnp.exp(draws), extent[axis_at] // shards_of).reshape((-1,) + (1,) * (len(extent) - 1 - axis_at))
    return level


def bell_draw(own_key, dims, deviation, reach, shards=(), kind=jnp.bfloat16):
    loudness = shard_levels(own_key, dims, shards, -0.22, 0.18) if shards else 1.0
    values = jax.random.normal(own_key, dims, jnp.float32) * deviation * loudness
    return jnp.minimum(jnp.maximum(values, -reach), reach).astype(kind)


def setup_inputs(seed: int = 0, part: int = 0) -> dict:
    seeds = jax.random.split(jax.random.key(seed), 10)
    part_keys = jax.random.split(jax.random.fold_in(seeds[9], part), 10)
    prefix_q = draw_prefix_q(jax.random.fold_in(jax.random.fold_in(seeds[9], part), 71), part)
    prefix_k = draw_prefix_k(jax.random.fold_in(jax.random.fold_in(seeds[9], part), 71), part)
    prefix_v = bell_draw(part_keys[2], (PREFIX, KVH * HD), 1.0, 6.0, ((0, 16), (1, 4)))
    resp_q = draw_resp_q(jax.random.fold_in(jax.random.fold_in(seeds[9], part), 71), part)
    resp_k = bell_draw(part_keys[4], (N_GRP, R_MAX, KVH * HD), 1.0, 6.0, ((0, 16), (2, 4)))
    resp_v = bell_draw(part_keys[5], (N_GRP, R_MAX, KVH * HD), 1.0, 6.0, ((0, 16), (2, 4)))
    lengths = draw_lengths(jax.random.fold_in(jax.random.fold_in(seeds[9], part), 71), part)
    d_prefix_out = bell_draw(part_keys[7], (PREFIX, HQ * HD), 1.0, 6.0, ((0, 16), (1, 4)))
    d_resp_out = bell_draw(part_keys[8], (N_GRP, R_MAX, HQ * HD), 1.0, 6.0, ((0, 16), (2, 4)))
    return dict(prefix_q=prefix_q, prefix_k=prefix_k, prefix_v=prefix_v, resp_q=resp_q, resp_k=resp_k, resp_v=resp_v, lengths=lengths, d_prefix_out=d_prefix_out, d_resp_out=d_resp_out)


masked_value = -1e+30

def attend(queries, keys, values, out_grads, visible):
    query_count = queries.shape[0]
    key_count = keys.shape[0]
    per_group = HQ // KVH
    scale = 1.0 / math.sqrt(HD)
    query_four = queries.astype(jnp.float32).reshape(query_count, KVH, per_group, HD)
    key_three = keys.astype(jnp.float32).reshape(key_count, KVH, HD)
    value_three = values.astype(jnp.float32).reshape(key_count, KVH, HD)
    grad_four = out_grads.astype(jnp.float32).reshape(query_count, KVH, per_group, HD).transpose(1, 2, 0, 3)
    logits = jnp.einsum('qhgd,khd->hgqk', query_four, key_three) * scale
    logits = jnp.where(visible[None, None], logits, masked_value)
    row_max = lax.optimization_barrier(jnp.max(logits, -1, keepdims=True))
    exponent = jnp.exp(logits - row_max)
    row_sum = lax.optimization_barrier(jnp.sum(exponent, -1, keepdims=True))
    weights = exponent / row_sum
    weights_low = lax.optimization_barrier(weights.astype(jnp.bfloat16)).astype(jnp.float32)
    attended = jnp.einsum('hgqk,khd->hgqd', weights_low, value_three)
    attended = lax.optimization_barrier(attended.astype(jnp.bfloat16)).astype(jnp.float32)
    row_dot = lax.optimization_barrier(jnp.sum(grad_four * attended, -1, keepdims=True))
    grad_logit = jnp.einsum('hgqd,khd->hgqk', grad_four, value_three)
    logit_grad = weights * (grad_logit - row_dot)
    logit_low = lax.optimization_barrier(logit_grad.astype(jnp.bfloat16)).astype(jnp.float32)
    query_grad = jnp.einsum('hgqk,khd->qhgd', logit_low, key_three) * scale
    key_grad = jnp.einsum('hgqk,qhgd->khd', logit_low, query_four) * scale
    value_grad = jnp.einsum('hgqk,hgqd->khd', weights_low, grad_four)
    return (query_grad.reshape(query_count, HQ * HD).astype(jnp.bfloat16), key_grad.reshape(key_count, KVH * HD), value_grad.reshape(key_count, KVH * HD))

def reference(prefix_q, prefix_k, prefix_v, resp_q, resp_k, resp_v, lengths, d_prefix_out, d_resp_out):
    prefix_pos = jnp.arange(PREFIX)
    prefix_visible = prefix_pos[None, :] <= prefix_pos[:, None]
    prefix_qgrad, prefix_kgrad, prefix_vgrad = attend(prefix_q, prefix_k, prefix_v, d_prefix_out, prefix_visible)
    positions = jnp.arange(R_MAX)
    resp_visible = jnp.concatenate([jnp.ones((R_MAX, PREFIX), bool), positions[None, :] <= positions[:, None]], 1)

    def scan_step(carry, item):
        query_rows, key_rows, value_rows, length, grad_rows = item
        live = positions < length
        grad_rows = jnp.where(live[:, None], grad_rows, jnp.zeros_like(grad_rows))
        keys_all = jnp.concatenate([prefix_k, key_rows], 0)
        values_all = jnp.concatenate([prefix_v, value_rows], 0)
        query_grad, key_grad, value_grad = attend(query_rows, keys_all, values_all, grad_rows, resp_visible)
        carry = (carry[0] + key_grad[:PREFIX], carry[1] + value_grad[:PREFIX])
        return (carry, (query_grad, key_grad[PREFIX:].astype(jnp.bfloat16), value_grad[PREFIX:].astype(jnp.bfloat16)))
    sums, stacked = lax.scan(scan_step, (prefix_kgrad, prefix_vgrad), (resp_q, resp_k, resp_v, lengths, d_resp_out))
    return (prefix_qgrad, sums[0].astype(jnp.bfloat16), sums[1].astype(jnp.bfloat16), stacked[0], stacked[1], stacked[2])
```

```python
import math

import jax
import jax.numpy as jnp
from jax import lax
from jax.experimental import pallas as pl
from jax.experimental.pallas import tpu as pltpu
from jax.sharding import PartitionSpec as P

HQ = 64
KVH = 8
HD = 128
per_group = HQ // KVH
scale = 1.0 / math.sqrt(HD)
scale_log2 = scale * math.log2(math.e)
masked_value = -1e30
unit = 256
step = 64
low = jnp.bfloat16


def dot(a, b):
    return jnp.dot(a, b, preferred_element_type=jnp.float32)


def dot_rows(a, b):
    return lax.dot_general(a, b, (((1,), (1,)), ((), ())), preferred_element_type=jnp.float32)


def together(copies):
    for copy in copies:
        copy.start()
    for copy in copies:
        copy.wait()


def spread_body(k, v, out, block, sems):
    rows, columns = k.shape
    block[:, 0:columns] = k[...]
    block[:, columns : 2 * columns] = v[...]
    together(
        [
            pltpu.make_async_copy(block, out.at[d * rows : (d + 1) * rows, :], sems.at[d])
            for d in range(out.shape[0] // rows)
        ]
    )


def stack_body(info, pq, rq, pdo, rdo, rk, rv, qs, dos, own, query_pos, qs_out, dos_out, sems):
    resp_rows = rq.shape[0]
    prefix_rows = pq.shape[0]
    span = per_group * (resp_rows + prefix_rows)
    columns = rk.shape[1]
    moves = [(rk, own.at[:, 0:columns]), (rv, own.at[:, columns : 2 * columns])]
    for h in range(pq.shape[1] // HD):
        part = slice(h * HD, (h + 1) * HD)
        first = h // per_group * span + h % per_group * resp_rows
        at = slice(first, first + resp_rows)
        moves += [(rq.at[:, part], qs.at[at, :]), (rdo.at[:, part], dos.at[at, :])]
        first = h // per_group * span + per_group * resp_rows + h % per_group * prefix_rows
        at = slice(first, first + prefix_rows)
        moves += [(pq.at[:, part], qs.at[at, :]), (pdo.at[:, part], dos.at[at, :])]
    together([pltpu.make_async_copy(a, b, sems.at[i]) for i, (a, b) in enumerate(moves)])
    live = lax.broadcasted_iota(jnp.int32, (resp_rows, HD), 0) < info[1]
    for h in range(pq.shape[1] // HD):
        first = h // per_group * span + h % per_group * resp_rows
        at = slice(first, first + resp_rows)
        dos[at, :] = jnp.where(live, dos[at, :], jnp.zeros((), low))
    together([pltpu.make_async_copy(a, b, sems.at[i]) for i, (a, b) in enumerate(((qs, qs_out), (dos, dos_out)))])
    query_pos[...] = info[0] + lax.broadcasted_iota(jnp.int32, query_pos.shape, 1) % prefix_rows


def hide_later(logits, at, prefix_total, is_resp, resp_rows, query_pos):
    if is_resp and at < prefix_total:
        return logits
    key_pos = lax.broadcasted_iota(jnp.int32, logits.shape, 0)
    if is_resp:
        last = lax.broadcasted_iota(jnp.int32, logits.shape, 1) % resp_rows - (at - prefix_total)
    else:
        last = query_pos[0:1, :] - at
    return jnp.where(key_pos <= last, logits, masked_value)


def attend_body(resp_all, kv, own, qs, dos, query_pos, terms, stats, ps, ds, dkv, s_ref, g_ref, qi, doi, ks, vs, sems):
    prefix_total = kv.shape[0]
    resp_rows = own.shape[0]
    columns = own.shape[1] // 2
    key_count = prefix_total + resp_rows
    heads = columns // HD
    row_count = qs.shape[0] // heads
    copies = []

    def send(columns):
        copy = pltpu.make_async_copy(dkv.at[:, columns], terms.at[:, columns], sems.at[len(copies)])
        copy.start()
        copies.append(copy)

    def fold(x):
        return jnp.sum(x.reshape(x.shape[0] // 8, 8, unit), 0)

    for h in range(heads):
        k_at = slice(h * HD, (h + 1) * HD)
        v_at = slice(columns + h * HD, columns + (h + 1) * HD)
        ks[h, 0:prefix_total, :] = kv[:, k_at]
        ks[h, prefix_total:, :] = own[:, k_at]
        vs[h, 0:prefix_total, :] = kv[:, v_at]
        vs[h, prefix_total:, :] = own[:, v_at]
        for start in range(0, row_count, unit):
            rows = slice(start, start + unit)
            slot = start // unit % 2
            is_resp = start < resp_all
            count = key_count if is_resp else prefix_total
            query = qs[h * row_count + start : h * row_count + start + unit, :]
            out_grad = dos[h * row_count + start : h * row_count + start + unit, :]
            logits = dot_rows(ks[h, 0:count, :], query)
            top = None
            for at in range(0, count, step):
                part = logits[at : at + step]
                part = hide_later(part, at, prefix_total, is_resp, resp_rows, query_pos)
                s_ref[slot, at : at + step, :] = part
                here = jnp.max(part.reshape(step // 8, 8, unit), 0)
                top = here if top is None else jnp.maximum(top, here)
            g_ref[slot, 0:count, :] = dot_rows(vs[h, 0:count, :], out_grad)
            shift = jnp.max(top, 0, keepdims=True) * scale_log2
            row_sum = jnp.zeros((8, unit), jnp.float32)
            row_dot = jnp.zeros((8, unit), jnp.float32)
            for at in range(0, count, step):
                exponent = jnp.exp2(s_ref[slot, at : at + step, :] * scale_log2 - shift)
                row_sum += fold(exponent)
                row_dot += fold(exponent * g_ref[slot, at : at + step, :])
                if at < prefix_total:
                    ps[h, at : at + step, rows] = exponent.astype(low)
            inverse = 1.0 / jnp.sum(row_sum, 0, keepdims=True)
            row_dot = jnp.sum(row_dot, 0, keepdims=True) * inverse
            stats[8 * h : 8 * h + 1, rows] = shift
            stats[8 * h + 1 : 8 * h + 2, rows] = inverse
            stats[8 * h + 2 : 8 * h + 3, rows] = row_dot
            by_row = jnp.broadcast_to(inverse, (HD, unit)).T
            qi[h, rows, :] = (query.astype(jnp.float32) * by_row).astype(low)
            doi[h, rows, :] = (out_grad.astype(jnp.float32) * by_row).astype(low)
            for at in range(0, prefix_total, step):
                exponent = ps[h, at : at + step, rows].astype(jnp.float32)
                ds[h, at : at + step, rows] = (exponent * (g_ref[slot, at : at + step, :] - row_dot)).astype(low)
        dkv[:, v_at] = dot(ps[h], doi[h]).astype(low)
        send(v_at)
        dkv[:, k_at] = (dot(ds[h], qi[h]) * scale).astype(low)
        send(k_at)
    for copy in copies:
        copy.wait()


def finish_body(resp_all, kv, own, query_pos, stats, qs_in, dos_in, dpq, drq, drk, drv, qs, dos, ks, vs, kt, pw, dw, sems):
    together([pltpu.make_async_copy(a, b, sems.at[i]) for i, (a, b) in enumerate(((qs_in, qs), (dos_in, dos)))])
    prefix_total = kv.shape[0]
    resp_rows = own.shape[0]
    columns = own.shape[1] // 2
    heads = columns // HD
    row_count = qs.shape[0] // heads
    prefix_rows = dpq.shape[0]
    for h in range(heads):
        k_at = slice(h * HD, (h + 1) * HD)
        v_at = slice(columns + h * HD, columns + (h + 1) * HD)
        ks[0:prefix_total, :] = kv[:, k_at]
        ks[prefix_total:, :] = own[:, k_at]
        vs[0:prefix_total, :] = kv[:, v_at]
        vs[prefix_total:, :] = own[:, v_at]
        kt[...] = ks[...].T
        for start in range(0, row_count, unit):
            rows = slice(start, start + unit)
            is_resp = start < resp_all
            count = prefix_total + resp_rows if is_resp else prefix_total
            shift = stats[8 * h : 8 * h + 1, rows]
            inverse = stats[8 * h + 1 : 8 * h + 2, rows]
            row_dot = stats[8 * h + 2 : 8 * h + 3, rows]
            logits = dot_rows(ks[0:count, :], qs[h * row_count + start : h * row_count + start + unit, :])
            grad_logit = dot_rows(vs[0:count, :], dos[h * row_count + start : h * row_count + start + unit, :])
            slopes = []
            for at in range(0, count, step):
                part = hide_later(logits[at : at + step], at, prefix_total, is_resp, resp_rows, query_pos)
                weights = jnp.exp2(part * scale_log2 - shift) * inverse
                slope = (weights * (grad_logit[at : at + step] - row_dot)).astype(low)
                slopes.append(slope)
                if at >= prefix_total:
                    pw[at - prefix_total : at - prefix_total + step, rows] = weights.astype(low)
                    dw[at - prefix_total : at - prefix_total + step, rows] = slope
            grad = (dot(kt[:, 0:count], jnp.concatenate(slopes, 0)) * scale).astype(low).T
            if is_resp:
                out, size, first = drq, resp_rows, start
            else:
                out, size, first = dpq, prefix_rows, start - resp_all
            for j in range(unit // size):
                head = h * per_group + first // size + j
                out[:, head * HD : (head + 1) * HD] = grad[j * size : (j + 1) * size]
        span = slice(h * row_count, h * row_count + resp_all)
        drv[:, k_at] = dot(pw[...], dos[span, :]).astype(low)
        drk[:, k_at] = (dot(dw[...], qs[span, :]) * scale).astype(low)


def total_body(parts, k, v):
    rows, columns = k.shape
    total = parts[0:rows, :].astype(jnp.float32)
    for d in range(1, parts.shape[0] // rows):
        total += parts[d * rows : (d + 1) * rows, :].astype(jnp.float32)
    total = total.astype(low)
    k[...] = total[:, 0:columns]
    v[...] = total[:, columns : 2 * columns]


def array(*shape):
    return jax.ShapeDtypeStruct(shape, low)


anywhere = pl.BlockSpec(memory_space=pl.ANY)
near = pl.BlockSpec(memory_space=pltpu.VMEM)
scalars = pl.BlockSpec(memory_space=pltpu.SMEM)
params = pltpu.CompilerParams(vmem_limit_bytes=30 * 1024 * 1024)


def exchange(blocks):
    return lax.all_to_all(blocks, "grp", 0, 0, tiled=True)


def on_device(
    prefix_q, prefix_k, prefix_v, resp_q, resp_k, resp_v, lengths, d_prefix_out, d_resp_out
):
    devices = lax.axis_size("grp")
    prefix_rows, columns = prefix_k.shape
    resp_rows = resp_q.shape[1]
    heads = columns // HD
    prefix_total = devices * prefix_rows
    key_count = prefix_total + resp_rows
    resp_all = per_group * resp_rows
    row_count = resp_all + per_group * prefix_rows
    info = jnp.stack([lax.axis_index("grp").astype(jnp.int32) * prefix_rows, lengths[0]])
    spread = pl.pallas_call(
        spread_body,
        in_specs=[near] * 2,
        out_specs=anywhere,
        out_shape=pltpu.HBM((prefix_total, 2 * columns), low),
        scratch_shapes=[pltpu.VMEM((prefix_rows, 2 * columns), low), pltpu.SemaphoreType.DMA((devices,))],
        name="spread",
    )(prefix_k, prefix_v)
    kv = exchange(spread)
    qs, dos, own, query_pos, qs_far, dos_far = pl.pallas_call(
        stack_body,
        in_specs=[scalars] + [anywhere] * 6,
        out_specs=[near] * 4 + [anywhere] * 2,
        out_shape=[
            pltpu.VMEM((heads * row_count, HD), low),
            pltpu.VMEM((heads * row_count, HD), low),
            pltpu.VMEM((resp_rows, 2 * columns), low),
            pltpu.VMEM((8, unit), jnp.int32),
            pltpu.HBM((heads * row_count, HD), low),
            pltpu.HBM((heads * row_count, HD), low),
        ],
        scratch_shapes=[pltpu.SemaphoreType.DMA((2 + 4 * heads * per_group,))],
        name="stack",
    )(info, prefix_q, resp_q[0], d_prefix_out, d_resp_out[0], resp_k[0], resp_v[0])
    terms, stats = pl.pallas_call(
        lambda *refs: attend_body(resp_all, *refs),
        in_specs=[near] * 5,
        out_specs=[anywhere, near],
        out_shape=[
            pltpu.HBM((prefix_total, 2 * columns), low),
            jax.ShapeDtypeStruct((8 * heads, row_count), jnp.float32),
        ],
        scratch_shapes=[
            pltpu.VMEM((heads, prefix_total, row_count), low),
            pltpu.VMEM((heads, prefix_total, row_count), low),
            pltpu.VMEM((prefix_total, 2 * columns), low),
            pltpu.VMEM((2, key_count, unit), jnp.float32),
            pltpu.VMEM((2, key_count, unit), jnp.float32),
            pltpu.VMEM((heads, row_count, HD), low),
            pltpu.VMEM((heads, row_count, HD), low),
            pltpu.VMEM((heads, key_count, HD), low),
            pltpu.VMEM((heads, key_count, HD), low),
            pltpu.SemaphoreType.DMA((2 * heads,)),
        ],
        compiler_params=params,
        name="attend",
    )(kv, own, qs, dos, query_pos)
    parts = exchange(terms)
    grad_prefix_q, grad_resp_q, grad_resp_k, grad_resp_v = pl.pallas_call(
        lambda *refs: finish_body(resp_all, *refs),
        in_specs=[near] * 4 + [anywhere] * 2,
        out_specs=[near] * 4,
        out_shape=[array(*prefix_q.shape), array(*resp_q.shape[1:])] + [array(resp_rows, columns)] * 2,
        scratch_shapes=[
            pltpu.VMEM((heads * row_count, HD), low),
            pltpu.VMEM((heads * row_count, HD), low),
            pltpu.VMEM((key_count, HD), low),
            pltpu.VMEM((key_count, HD), low),
            pltpu.VMEM((HD, key_count), low),
            pltpu.VMEM((resp_rows, resp_all), low),
            pltpu.VMEM((resp_rows, resp_all), low),
            pltpu.SemaphoreType.DMA((2,)),
        ],
        compiler_params=params,
        name="finish",
    )(kv, own, query_pos, stats, qs_far, dos_far)
    grad_prefix_k, grad_prefix_v = pl.pallas_call(
        total_body, in_specs=[near], out_specs=[near] * 2, out_shape=[array(prefix_rows, columns)] * 2, name="total"
    )(pltpu.with_memory_space_constraint(parts, pltpu.VMEM))
    return (grad_prefix_q, grad_prefix_k, grad_prefix_v, grad_resp_q[None], grad_resp_k[None], grad_resp_v[None])


def solution(mesh):
    rows = P(("batch", "grp"), "tp")
    items = P(("batch", "grp"), None, "tp")
    return jax.shard_map(
        on_device,
        mesh=mesh,
        in_specs=(rows, rows, rows, items, items, items, P(("batch", "grp")), rows, items),
        out_specs=(rows, rows, rows, items, items, items),
        check_vma=False,
    )
```

```python
import math

import jax
import jax.numpy as jnp
from jax import lax
from jax.experimental import pallas as pl
from jax.experimental.pallas import tpu as pltpu
from jax.sharding import PartitionSpec as P

HQ = 64
KVH = 8
HD = 128
per_group = HQ // KVH
scale = 1.0 / math.sqrt(HD)
scale_log2 = scale * math.log2(math.e)
masked_value = -1e30
unit = 256
step = 64
PIECES = 1
GATHER = 1
low = jnp.bfloat16


def dot(a, b):
    return jnp.dot(a, b, preferred_element_type=jnp.float32)


def dot_rows(a, b):
    return lax.dot_general(a, b, (((1,), (1,)), ((), ())), preferred_element_type=jnp.float32)


def together(copies):
    for copy in copies:
        copy.start()
    for copy in copies:
        copy.wait()


def spread_body(k, v, out, block, sems):
    rows, columns = k.shape
    devices = out.shape[0] // rows
    together(
        [
            pltpu.make_async_copy(k, block.at[:, 0:columns], sems.at[devices]),
            pltpu.make_async_copy(v, block.at[:, columns : 2 * columns], sems.at[devices + 1]),
        ]
    )
    together([pltpu.make_async_copy(block, out.at[d * rows : (d + 1) * rows, :], sems.at[d]) for d in range(devices)])


def stack_body(info, pq, rq, pdo, rdo, rk, rv, qs, dos, own, query_pos, qs_out, dos_out, sems):
    resp_rows = rq.shape[0]
    prefix_rows = pq.shape[0]
    span = per_group * (resp_rows + prefix_rows)
    columns = rk.shape[1]
    moves = [(rk, own.at[:, 0:columns]), (rv, own.at[:, columns : 2 * columns])]
    for h in range(pq.shape[1] // HD):
        part = slice(h * HD, (h + 1) * HD)
        first = h // per_group * span + h % per_group * resp_rows
        at = slice(first, first + resp_rows)
        moves += [(rq.at[:, part], qs.at[at, :]), (rdo.at[:, part], dos.at[at, :])]
        first = h // per_group * span + per_group * resp_rows + h % per_group * prefix_rows
        at = slice(first, first + prefix_rows)
        moves += [(pq.at[:, part], qs.at[at, :]), (pdo.at[:, part], dos.at[at, :])]
    together([pltpu.make_async_copy(a, b, sems.at[i]) for i, (a, b) in enumerate(moves)])
    live = lax.broadcasted_iota(jnp.int32, (resp_rows, HD), 0) < info[1]
    for h in range(pq.shape[1] // HD):
        first = h // per_group * span + h % per_group * resp_rows
        at = slice(first, first + resp_rows)
        dos[at, :] = jnp.where(live, dos[at, :], jnp.zeros((), low))
    together([pltpu.make_async_copy(a, b, sems.at[i]) for i, (a, b) in enumerate(((qs, qs_out), (dos, dos_out)))])
    query_pos[...] = info[0] + lax.broadcasted_iota(jnp.int32, query_pos.shape, 1) % prefix_rows


def hide_later(logits, at, prefix_total, is_resp, resp_rows, query_pos):
    if is_resp and at < prefix_total:
        return logits
    key_pos = lax.broadcasted_iota(jnp.int32, logits.shape, 0)
    if is_resp:
        last = lax.broadcasted_iota(jnp.int32, logits.shape, 1) % resp_rows - (at - prefix_total)
    else:
        last = query_pos[0:1, :] - at
    return jnp.where(key_pos <= last, logits, masked_value)


def attend_body(resp_all, kv, own, qs, dos, query_pos, terms, stats_out, stats, ps, ds, dkv, s_ref, g_ref, qi, doi, ks, vs, sems):
    prefix_total = kv.shape[0]
    resp_rows = own.shape[0]
    columns = own.shape[1] // 2
    key_count = prefix_total + resp_rows
    heads = columns // HD
    row_count = qs.shape[0] // heads
    units = [(h, start) for h in range(heads) for start in range(0, row_count, unit)]
    tops = {}
    copies = []

    def send(columns):
        copy = pltpu.make_async_copy(dkv.at[:, columns], terms.at[:, columns], sems.at[len(copies)])
        copy.start()
        copies.append(copy)

    def fold(x):
        return jnp.sum(x.reshape(x.shape[0] // 8, 8, unit), 0)

    def k_at(h):
        return slice(h * HD, (h + 1) * HD)

    def v_at(h):
        return slice(columns + h * HD, columns + (h + 1) * HD)

    def count_of(u):
        return key_count if units[u][1] < resp_all else prefix_total

    def rows_of(u):
        first = units[u][0] * row_count + units[u][1]
        return slice(first, first + unit)

    def products(u):
        h, start = units[u]
        slot = u % 2
        count = count_of(u)
        size = count // PIECES

        def logits_of(first):
            logits = dot_rows(ks[h, first : first + size, :], qs[rows_of(u), :])
            for at in range(first, first + size, step):
                part = logits[at - first : at - first + step]
                part = hide_later(part, at, prefix_total, start < resp_all, resp_rows, query_pos)
                s_ref[slot, at : at + step, :] = part
                here = jnp.max(part.reshape(step // 8, 8, unit), 0)
                tops[u] = jnp.maximum(tops[u], here) if u in tops else here

        def grads_of(first):
            g_ref[slot, first : first + size, :] = dot_rows(vs[h, first : first + size, :], dos[rows_of(u), :])

        for first in range(0, count, size):
            yield lambda first=first: logits_of(first)
        for first in range(0, count, size):
            yield lambda first=first: grads_of(first)

    def weigh(u):
        h, start = units[u]
        slot = u % 2
        rows = slice(start, start + unit)
        shift = jnp.max(tops[u], 0, keepdims=True) * scale_log2
        sums = [jnp.zeros((8, unit), jnp.float32), jnp.zeros((8, unit), jnp.float32)]

        def exponents_of(at):
            exponent = jnp.exp2(s_ref[slot, at : at + step, :] * scale_log2 - shift)
            sums[0] += fold(exponent)
            sums[1] += fold(exponent * g_ref[slot, at : at + step, :])
            if at < prefix_total:
                ps[h, at : at + step, rows] = exponent.astype(low)

        def close():
            inverse = 1.0 / jnp.sum(sums[0], 0, keepdims=True)
            row_dot = jnp.sum(sums[1], 0, keepdims=True) * inverse
            stats[8 * h : 8 * h + 1, rows] = shift
            stats[8 * h + 1 : 8 * h + 2, rows] = inverse
            stats[8 * h + 2 : 8 * h + 3, rows] = row_dot
            by_row = jnp.broadcast_to(inverse, (HD, unit)).T
            qi[h, rows, :] = (qs[rows_of(u), :].astype(jnp.float32) * by_row).astype(low)
            doi[h, rows, :] = (dos[rows_of(u), :].astype(jnp.float32) * by_row).astype(low)
            sums.append(row_dot)

        def slopes_of(at):
            exponent = ps[h, at : at + step, rows].astype(jnp.float32)
            ds[h, at : at + step, rows] = (exponent * (g_ref[slot, at : at + step, :] - sums[2])).astype(low)

        for at in range(0, count_of(u), step):
            yield lambda at=at: exponents_of(at)
        yield close
        for at in range(0, prefix_total, step):
            yield lambda at=at: slopes_of(at)

    def gather(h):
        size = prefix_total // GATHER

        def values_of(at):
            dkv[at : at + size, v_at(h)] = dot(ps[h, at : at + size, :], doi[h]).astype(low)

        def keys_of(at):
            dkv[at : at + size, k_at(h)] = (dot(ds[h, at : at + size, :], qi[h]) * scale).astype(low)

        for at in range(0, prefix_total, size):
            yield lambda at=at: values_of(at)
        yield lambda: send(v_at(h))
        for at in range(0, prefix_total, size):
            yield lambda at=at: keys_of(at)
        yield lambda: send(k_at(h))

    def weave(one, other):
        one, other = list(one), list(other)
        done = 0
        for i, task in enumerate(one):
            task()
            until = (i + 1) * len(other) // len(one)
            for j in range(done, until):
                other[j]()
            done = until

    for h in range(heads):
        ks[h, 0:prefix_total, :] = kv[:, k_at(h)]
        ks[h, prefix_total:, :] = own[:, k_at(h)]
        vs[h, 0:prefix_total, :] = kv[:, v_at(h)]
        vs[h, prefix_total:, :] = own[:, v_at(h)]
    for task in products(0):
        task()
    waiting = []
    per_head = row_count // unit
    for u in range(len(units)):
        h = units[u][0]
        beside = list(products(u + 1)) if u + 1 < len(units) else []
        left = (h + 1) * per_head - u
        take = -(-len(waiting) // left)
        beside += waiting[:take]
        waiting = waiting[take:]
        if beside:
            weave(weigh(u), beside)
        else:
            for task in weigh(u):
                task()
        if left == 1:
            waiting += list(gather(h))
    keep = pltpu.make_async_copy(stats, stats_out, sems.at[2 * heads])
    keep.start()
    for task in waiting:
        task()
    for copy in copies:
        copy.wait()
    keep.wait()


def finish_body(resp_all, kv, own, query_pos, stats, qs_in, dos_in, dpq, drq, drk, drv, qs, dos, ks, vs, kt, pw, dw, sems):
    together([pltpu.make_async_copy(a, b, sems.at[i]) for i, (a, b) in enumerate(((qs_in, qs), (dos_in, dos)))])
    prefix_total = kv.shape[0]
    resp_rows = own.shape[0]
    columns = own.shape[1] // 2
    heads = columns // HD
    row_count = qs.shape[0] // heads
    prefix_rows = dpq.shape[0]
    for h in range(heads):
        k_at = slice(h * HD, (h + 1) * HD)
        v_at = slice(columns + h * HD, columns + (h + 1) * HD)
        ks[0:prefix_total, :] = kv[:, k_at]
        ks[prefix_total:, :] = own[:, k_at]
        vs[0:prefix_total, :] = kv[:, v_at]
        vs[prefix_total:, :] = own[:, v_at]
        kt[...] = ks[...].T
        for start in range(0, row_count, unit):
            rows = slice(start, start + unit)
            is_resp = start < resp_all
            count = prefix_total + resp_rows if is_resp else prefix_total
            shift = stats[8 * h : 8 * h + 1, rows]
            inverse = stats[8 * h + 1 : 8 * h + 2, rows]
            row_dot = stats[8 * h + 2 : 8 * h + 3, rows]
            logits = dot_rows(ks[0:count, :], qs[h * row_count + start : h * row_count + start + unit, :])
            grad_logit = dot_rows(vs[0:count, :], dos[h * row_count + start : h * row_count + start + unit, :])
            slopes = []
            for at in range(0, count, step):
                part = hide_later(logits[at : at + step], at, prefix_total, is_resp, resp_rows, query_pos)
                weights = jnp.exp2(part * scale_log2 - shift) * inverse
                slope = (weights * (grad_logit[at : at + step] - row_dot)).astype(low)
                slopes.append(slope)
                if at >= prefix_total:
                    pw[at - prefix_total : at - prefix_total + step, rows] = weights.astype(low)
                    dw[at - prefix_total : at - prefix_total + step, rows] = slope
            grad = (dot(kt[:, 0:count], jnp.concatenate(slopes, 0)) * scale).astype(low).T
            if is_resp:
                out, size, first = drq, resp_rows, start
            else:
                out, size, first = dpq, prefix_rows, start - resp_all
            for j in range(unit // size):
                head = h * per_group + first // size + j
                out[:, head * HD : (head + 1) * HD] = grad[j * size : (j + 1) * size]
        span = slice(h * row_count, h * row_count + resp_all)
        drv[:, k_at] = dot(pw[...], dos[span, :]).astype(low)
        drk[:, k_at] = (dot(dw[...], qs[span, :]) * scale).astype(low)


def total_body(parts, k, v):
    rows, columns = k.shape
    total = parts[0:rows, :].astype(jnp.float32)
    for d in range(1, parts.shape[0] // rows):
        total += parts[d * rows : (d + 1) * rows, :].astype(jnp.float32)
    total = total.astype(low)
    k[...] = total[:, 0:columns]
    v[...] = total[:, columns : 2 * columns]


def array(*shape):
    return jax.ShapeDtypeStruct(shape, low)


anywhere = pl.BlockSpec(memory_space=pl.ANY)
near = pl.BlockSpec(memory_space=pltpu.VMEM)
scalars = pl.BlockSpec(memory_space=pltpu.SMEM)
params = pltpu.CompilerParams(vmem_limit_bytes=30 * 1024 * 1024)


def exchange(blocks):
    return lax.all_to_all(blocks, "grp", 0, 0, tiled=True)


def on_device(
    prefix_q, prefix_k, prefix_v, resp_q, resp_k, resp_v, lengths, d_prefix_out, d_resp_out
):
    devices = lax.axis_size("grp")
    prefix_rows, columns = prefix_k.shape
    resp_rows = resp_q.shape[1]
    heads = columns // HD
    prefix_total = devices * prefix_rows
    key_count = prefix_total + resp_rows
    resp_all = per_group * resp_rows
    row_count = resp_all + per_group * prefix_rows
    info = jnp.stack([lax.axis_index("grp").astype(jnp.int32) * prefix_rows, lengths[0]])
    spread = pl.pallas_call(
        spread_body,
        in_specs=[anywhere] * 2,
        out_specs=anywhere,
        out_shape=pltpu.HBM((prefix_total, 2 * columns), low),
        scratch_shapes=[pltpu.VMEM((prefix_rows, 2 * columns), low), pltpu.SemaphoreType.DMA((devices + 2,))],
        name="spread",
    )(prefix_k, prefix_v)
    kv = exchange(spread)
    qs, dos, own, query_pos, qs_far, dos_far = pl.pallas_call(
        stack_body,
        in_specs=[scalars] + [anywhere] * 6,
        out_specs=[near] * 4 + [anywhere] * 2,
        out_shape=[
            pltpu.VMEM((heads * row_count, HD), low),
            pltpu.VMEM((heads * row_count, HD), low),
            pltpu.VMEM((resp_rows, 2 * columns), low),
            pltpu.VMEM((8, unit), jnp.int32),
            pltpu.HBM((heads * row_count, HD), low),
            pltpu.HBM((heads * row_count, HD), low),
        ],
        scratch_shapes=[pltpu.SemaphoreType.DMA((2 + 4 * heads * per_group,))],
        name="stack",
    )(info, prefix_q, resp_q[0], d_prefix_out, d_resp_out[0], resp_k[0], resp_v[0])
    terms, stats = pl.pallas_call(
        lambda *refs: attend_body(resp_all, *refs),
        in_specs=[near] * 5,
        out_specs=[anywhere] * 2,
        out_shape=[
            pltpu.HBM((prefix_total, 2 * columns), low),
            pltpu.HBM((8 * heads, row_count), jnp.float32),
        ],
        scratch_shapes=[
            pltpu.VMEM((8 * heads, row_count), jnp.float32),
            pltpu.VMEM((heads, prefix_total, row_count), low),
            pltpu.VMEM((heads, prefix_total, row_count), low),
            pltpu.VMEM((prefix_total, 2 * columns), low),
            pltpu.VMEM((2, key_count, unit), jnp.float32),
            pltpu.VMEM((2, key_count, unit), jnp.float32),
            pltpu.VMEM((heads, row_count, HD), low),
            pltpu.VMEM((heads, row_count, HD), low),
            pltpu.VMEM((heads, key_count, HD), low),
            pltpu.VMEM((heads, key_count, HD), low),
            pltpu.SemaphoreType.DMA((2 * heads + 1,)),
        ],
        compiler_params=params,
        name="attend",
    )(kv, own, qs, dos, query_pos)
    parts = exchange(terms)
    grad_prefix_q, grad_resp_q, grad_resp_k, grad_resp_v = pl.pallas_call(
        lambda *refs: finish_body(resp_all, *refs),
        in_specs=[near] * 4 + [anywhere] * 2,
        out_specs=[near] * 4,
        out_shape=[array(*prefix_q.shape), array(*resp_q.shape[1:])] + [array(resp_rows, columns)] * 2,
        scratch_shapes=[
            pltpu.VMEM((heads * row_count, HD), low),
            pltpu.VMEM((heads * row_count, HD), low),
            pltpu.VMEM((key_count, HD), low),
            pltpu.VMEM((key_count, HD), low),
            pltpu.VMEM((HD, key_count), low),
            pltpu.VMEM((resp_rows, resp_all), low),
            pltpu.VMEM((resp_rows, resp_all), low),
            pltpu.SemaphoreType.DMA((2,)),
        ],
        compiler_params=params,
        name="finish",
    )(kv, own, query_pos, stats, qs_far, dos_far)
    grad_prefix_k, grad_prefix_v = pl.pallas_call(
        total_body, in_specs=[near], out_specs=[near] * 2, out_shape=[array(prefix_rows, columns)] * 2, name="total"
    )(pltpu.with_memory_space_constraint(parts, pltpu.VMEM))
    return (grad_prefix_q, grad_prefix_k, grad_prefix_v, grad_resp_q[None], grad_resp_k[None], grad_resp_v[None])


def solution(mesh):
    rows = P(("batch", "grp"), "tp")
    items = P(("batch", "grp"), None, "tp")
    return jax.shard_map(
        on_device,
        mesh=mesh,
        in_specs=(rows, rows, rows, items, items, items, P(("batch", "grp")), rows, items),
        out_specs=(rows, rows, rows, items, items, items),
        check_vma=False,
    )
```
